256 devices in a mesh: row: 8 (over z), col: 32 (over y, x, core).
Axes of the slice: x: 4, y: 4, z: 8, core: 2. Of those that a mesh axis runs over, the one named last changes fastest.
Arguments:
- tokens: bfloat16 [4096, 3200], P('row', 'col'), may hold values from -6 to 6
- pre_act: bfloat16 [4096, 12800], P('row', 'col'), may hold values from -5 to 5
- out_grad: bfloat16 [4096, 3200], P('row', 'col'), may hold values from -6 to 6
- up_weight: bfloat16 [3200, 12800], P('row', 'col'), may hold values from -0.21875 to 0.21875
- down_weight: bfloat16 [12800, 3200], P('col', 'row'), may hold values from -0.0546875 to 0.0546875
Outputs:
- tokens_grad: bfloat16 [4096, 3200], P('row', 'col')
- up_grad: float32 [3200, 12800], P('row', 'col')
- down_grad: float32 [12800, 3200], P('col', 'row')
The draws below stay inside these ranges and needn't reach their ends.
All inputs are finite; a program needn't handle non-finite values.
Results may differ from the reference program's by a relative error of at most 0.013.
Values may be sent and summed in bfloat16 or wider, within the bound.
No kernel may reach another device: no remote copies, remote signals or barrier semaphores. Data moves between devices by JAX's collectives and lax.ppermute only.
A program may use at most 128 MiB of HBM per device.

```python
import jax
import jax.numpy as jnp
from jax import lax

D = 3200
FF = 12800
TOKENS = 4096


def strengthened(result, rng, source, target, shards_of, factor):
    def block_of(dim):
        return (jnp.arange(result.shape[dim]) // (result.shape[dim] // shards_of)).reshape((-1,) + (1,) * (result.ndim - 1 - dim))

    first = jax.random.permutation(rng, shards_of)[block_of(target)]
    second = (block_of(target) + shards_of // 2) % shards_of
    return jnp.where((block_of(source) == first) | (block_of(source) == second), factor * result, result)


def block_scale(stream_key, extent, shards, least, high):
    gain, own = 1.0, jax.random.fold_in(stream_key, 6)
    for dim, parts in shards:
        draws = jnp.exp(jax.random.uniform(jax.random.fold_in(own, dim), (parts,), jnp.float32, least / len(shards), high / len(shards)))
        gain = gain * jnp.repeat(draws, extent[dim] // parts).reshape([-1 if axis == dim else 1 for axis in range(len(extent))])
    return gain


def gaussian(own_key, dims, deviation, reach, pieces=(), kind=jnp.bfloat16):
    gain = block_scale(own_key, dims, pieces, -0.22, 0.18) if pieces else 1.0
    drawn = jax.random.normal(own_key, dims, jnp.float32) * deviation * gain
    return jnp.minimum(jnp.maximum(drawn, -reach), reach).astype(kind)


def noise_with(stream_key, shape, deviation, reach, pieces, heavy, held_as=jnp.bfloat16):
    values = deviation * jax.random.normal(stream_key, shape, jnp.float32)
    if pieces:
        values = values * block_scale(stream_key, shape, pieces, -0.22, 0.18)
    return jnp.clip(strengthened(values, jax.random.fold_in(stream_key, 3), *heavy), -reach, reach).astype(held_as)


def setup_inputs(seed: int = 0) -> dict:
    arg_keys = jax.random.split(jax.random.key(seed), 6)
    tokens = noise_with(arg_keys[0], (TOKENS, D), 1.0, 6.0, ((0, 8), (1, 32)), (0, 1, 32, 2.75))
    pre_act = gaussian(arg_keys[1], (TOKENS, FF), 1.0, 5.0, ((0, 8), (1, 32)))
    out_grad = gaussian(arg_keys[2], (TOKENS, D), 1.0, 6.0, ((0, 8), (1, 32)))
    up_weight = noise_with(arg_keys[3], (D, FF), D ** -0.5, 0.21875, ((0, 8), (1, 32)), (1, 0, 32, 2.75))
    down_weight = gaussian(arg_keys[4], (FF, D), FF ** -0.5, 0.0546875, ((0, 32), (1, 8)))
    return dict(tokens=tokens, pre_act=pre_act, out_grad=out_grad, up_weight=up_weight, down_weight=down_weight)


INV_ROOT_TWO = 0.7071067811865476
INV_ROOT_TAU = 0.3989422804014327


def gelu_parts(pre_value):
    normal_cdf = 0.5 * (1.0 + lax.erf(pre_value * INV_ROOT_TWO))
    slope = normal_cdf + pre_value * jnp.exp(-0.5 * pre_value * pre_value) * INV_ROOT_TAU
    return pre_value * normal_cdf, slope


def reference(tokens, pre_act, out_grad, up_weight, down_weight):
    act_grad = jnp.dot(out_grad, down_weight.T, preferred_element_type=jnp.float32)
    pre_value = pre_act.astype(jnp.float32)
    act_value, slope = gelu_parts(pre_value)
    pre_grad = (act_grad * slope).astype(jnp.bfloat16)
    activated = act_value.astype(jnp.bfloat16)
    tokens_grad = jnp.dot(pre_grad, up_weight.T, preferred_element_type=jnp.float32).astype(jnp.bfloat16)
    up_grad = jnp.dot(tokens.T, pre_grad, preferred_element_type=jnp.float32)
    down_grad = jnp.dot(activated.T, out_grad, preferred_element_type=jnp.float32)
    return tokens_grad, up_grad, down_grad
```

```python
import jax
import jax.numpy as jnp
from jax import lax
from jax.sharding import PartitionSpec as P

INV_ROOT_TWO = 0.7071067811865476
INV_ROOT_TAU = 0.3989422804014327

ROWS = 8
COLS = 32
CHIPS = COLS // 2
WIDTH = 100
PADDED = 112

SAME_CORE = [[2 * chip + core for chip in range(CHIPS)] for core in range(2)]
CORE_SWAP = [(c, c ^ 1) for c in range(COLS)]
TO_SLAB = [
    (r * COLS + c, (c // 4) * COLS + 4 * r + c % 4) for r in range(ROWS) for c in range(COLS)
]


def gelu_parts(pre_value):
    normal_cdf = 0.5 * (1.0 + lax.erf(pre_value * INV_ROOT_TWO))
    slope = normal_cdf + pre_value * jnp.exp(-0.5 * pre_value * pre_value) * INV_ROOT_TAU
    return (pre_value * normal_cdf, slope)


def contract_last(left, right):
    return lax.dot_general(
        left, right, (((1,), (1,)), ((), ())), preferred_element_type=jnp.float32
    )


def matmul(left, right):
    return jnp.dot(left, right, preferred_element_type=jnp.float32)


def shift(block, step):
    return lax.ppermute(block, "row", [(i, (i + step) % ROWS) for i in range(ROWS)])


def ring(block):
    half = block.shape[0] // 2 // 16 * 16
    up = down = block
    found = [(0, block)]
    for step in range(1, 4):
        up, down = shift(up, 1), shift(down, -1)
        found += [(-step, up), (step, down)]
    far = jnp.concatenate([shift(up[:half], 1), shift(down[half:], -1)], axis=0)
    return found + [(4, far)]


def swap_cores(block):
    return lax.ppermute(block, "col", CORE_SWAP)


def to_chips(blocks):
    flat = blocks.reshape((CHIPS * PADDED,) + blocks.shape[2:])
    moved = lax.all_to_all(flat, "col", 0, 0, tiled=True, axis_index_groups=SAME_CORE)
    return moved.reshape(blocks.shape)


def per_device(tokens, pre_act, out_grad, up_weight, down_weight):
    row, core = lax.axis_index("row"), lax.axis_index("col") % 2
    room = ((0, PADDED - WIDTH), (0, 0))
    grad_t, tok_t = jnp.pad(out_grad.T, room), jnp.pad(tokens.T, room)

    slabs = lax.ppermute(jnp.stack([tok_t, grad_t]), ("row", "col"), TO_SLAB)
    slabs = lax.all_gather(slabs, "col", axis=0)
    slabs = slabs.reshape(ROWS, 4, 2, PADDED, -1)

    mine = to_chips(jnp.broadcast_to(grad_t[None], (CHIPS,) + grad_t.shape))
    other = swap_cores(mine)
    even, odd = jnp.where(core == 0, mine, other), jnp.where(core == 0, other, mine)
    grad_full = jnp.stack([even, odd], axis=1)[:, :, :WIDTH].reshape(ROWS, 4 * WIDTH, -1)

    act_grad = 0.0
    for offset, weight in ring(down_weight):
        block = lax.dynamic_index_in_dim(grad_full, (row + offset) % ROWS, 0, False)
        act_grad = act_grad + matmul(weight, block)

    up_full = jnp.zeros((ROWS,) + up_weight.shape, up_weight.dtype)
    for offset, weight in ring(up_weight):
        up_full = lax.dynamic_update_index_in_dim(up_full, weight, (row + offset) % ROWS, 0)

    pre_t = pre_act.T
    slope = gelu_parts(pre_t.astype(jnp.float32))[1]
    pre_grad = (act_grad * slope).astype(jnp.bfloat16)

    partial = matmul(up_full.reshape(-1, up_weight.shape[1]), pre_grad)
    partial = partial.reshape(CHIPS, 2, WIDTH, -1)
    keep = lax.dynamic_index_in_dim(partial, core, 1, False)
    send = lax.dynamic_index_in_dim(partial, 1 - core, 1, False).astype(jnp.bfloat16)
    pair = (keep + swap_cores(send).astype(jnp.float32)).astype(jnp.bfloat16)
    pair = jnp.pad(pair, ((0, 0),) + room)
    total = jnp.sum(to_chips(pair).astype(jnp.float32), axis=0)[:WIDTH]
    tokens_grad = total.T.astype(jnp.bfloat16)

    leading = 0.0
    for offset, block in ring(pre_grad):
        slab = lax.dynamic_index_in_dim(slabs, (row + offset) % ROWS, 0, False)[:, 0]
        leading = leading + contract_last(slab.reshape(4 * PADDED, -1), block)
    leading = leading.reshape(4, PADDED, -1)[:, :WIDTH].reshape(4 * WIDTH, -1)

    trailing = 0.0
    for offset, block in ring(pre_t):
        slab = lax.dynamic_index_in_dim(slabs, (row + offset) % ROWS, 0, False)[:, 1]
        act = gelu_parts(block.astype(jnp.float32))[0].astype(jnp.bfloat16)
        trailing = trailing + contract_last(slab.reshape(4 * PADDED, -1), act)
    trailing = trailing.reshape(4, PADDED, -1)[:, :WIDTH].reshape(4 * WIDTH, -1).T

    return (tokens_grad, leading, trailing)


def solution(mesh):
    in_specs = (P("row", "col"), P("row", "col"), P("row", "col"), P("row", "col"), P("col", "row"))
    out_specs = (P("row", "col"), P("row", "col"), P("col", "row"))
    return jax.shard_map(
        per_device, mesh=mesh, in_specs=in_specs, out_specs=out_specs, check_vma=False
    )
```

```python
import functools

import jax
import jax.numpy as jnp
from jax import lax
from jax.experimental import pallas as pl
from jax.experimental.pallas import tpu as pltpu
from jax.sharding import PartitionSpec as P

INV_ROOT_TWO = 0.7071067811865476
INV_ROOT_TAU = 0.3989422804014327

ROWS = 8
COLS = 32
CHIPS = COLS // 2
BLOCK = 512
SIDE = 400
WIDTH = 100
PADDED = 112
MAIN = 384
REST = SIDE - MAIN
PACKED = SIDE + 2 * REST
HALF = 224

SAME_CORE = [[2 * chip + core for chip in range(CHIPS)] for core in range(2)]
CORE_SWAP = [(c, c ^ 1) for c in range(COLS)]
OFFSETS = (0, -1, 1, -2, 2, -3, 3)


def gelu_parts(pre_value):
    normal_cdf = 0.5 * (1.0 + lax.erf(pre_value * INV_ROOT_TWO))
    slope = normal_cdf + pre_value * jnp.exp(-0.5 * pre_value * pre_value) * INV_ROOT_TAU
    return (pre_value * normal_cdf, slope)


def after(value, *earlier):
    return lax.optimization_barrier((value,) + earlier)[0]


def shift(block, step):
    return lax.ppermute(block, "row", [(i, (i + step) % ROWS) for i in range(ROWS)])


def gather_ring(block):
    up = down = block
    pieces = [block]
    for _ in range(3):
        up, down = shift(up, 1), shift(down, -1)
        pieces += [up, down]
    return pieces + [shift(up[:HALF], 1), shift(down[HALF:], -1)]


def sum_ring(parts):
    def plus(part, came):
        return (part.astype(jnp.float32) + came.astype(jnp.float32)).astype(part.dtype)

    up, down = shift(parts[4, :HALF], 1), shift(parts[4, HALF:], -1)
    up = jnp.concatenate([plus(parts[3, :HALF], up), parts[3, HALF:]], axis=0)
    down = jnp.concatenate([parts[5, :HALF], plus(parts[5, HALF:], down)], axis=0)
    for step in (2, 1):
        up, down = shift(up, 1), shift(down, -1)
        up, down = plus(parts[step], up), plus(parts[ROWS - step], down)
    up, down = shift(up, 1), shift(down, -1)
    total = parts[0].astype(jnp.float32) + up.astype(jnp.float32) + down.astype(jnp.float32)
    rest = jnp.concatenate([total[SIDE : SIDE + REST], total[SIDE + REST :, :REST]], axis=1)
    return jnp.concatenate([total[:SIDE], rest.T], axis=1)


def pack(block):
    rest = block[:, MAIN:].T
    corner = jnp.pad(rest[:, MAIN:], ((0, 0), (0, MAIN - REST)))
    return jnp.concatenate([block[:, :MAIN], rest[:, :MAIN], corner], axis=0)


def swap_cores(block):
    return lax.ppermute(block, "col", CORE_SWAP)


def to_chips(blocks):
    flat = blocks.reshape((-1,) + blocks.shape[2:])
    moved = lax.all_to_all(flat, "col", 0, 0, tiled=True, axis_index_groups=SAME_CORE)
    return moved.reshape(blocks.shape)


def dot(left, right, left_dim, right_dim):
    return lax.dot_general(
        left,
        right,
        (((left_dim,), (right_dim,)), ((), ())),
        preferred_element_type=jnp.float32,
    )


def each_row(here, pieces):
    for offset, piece in zip(OFFSETS, pieces):
        yield lax.rem(here[0] + (offset + ROWS), ROWS), piece[...]
    far = jnp.concatenate([pieces[7][...], pieces[8][...]], axis=0)
    yield lax.rem(here[0] + 4, ROWS), far


def times(total, weight, right):
    total[...] = dot(weight[:SIDE], right[:MAIN], 1, 0)
    add_rest(total, weight, right)


def add_rest(total, weight, right):
    total[:MAIN] += dot(weight[SIDE : SIDE + REST], right[MAIN:], 0, 0)
    corner = weight[SIDE + REST :, :128]
    total[MAIN:] += dot(corner, right[MAIN:], 0, 0)[:REST]


def order_kernel(here, own, other, out, tall):
    first = here[1] == 0
    for row in range(ROWS):
        for j in range(4):
            mine, their = own[2 * row + j // 2], other[2 * row + j // 2]
            if j % 2:
                mine, their = their, mine
            block = jnp.where(first, mine.astype(jnp.float32), their.astype(jnp.float32))
            tall[j * WIDTH : (j + 1) * WIDTH] = block[:WIDTH]
        out[row] = tall[...].astype(out.dtype)


def hidden_kernel(here, grad, slope, *rest):
    pieces, (out, total) = rest[:9], rest[9:]
    total[...] = jnp.zeros_like(total)
    for row, weight in each_row(here, pieces):
        right = grad[row]
        total[...] += dot(weight[:SIDE], right[:MAIN], 1, 0)
        add_rest(total, weight, right)
    out[...] = (total[...] * slope[...]).astype(out.dtype)


def input_kernel(own, here, pre_grad, *rest):
    pieces, (out, total) = rest[:9], rest[-2:]
    even = here[1] == (0 if own else 1)
    right = pre_grad[...]
    total[SIDE:] = jnp.zeros_like(total[SIDE:])
    for row, weight in each_row(here, pieces):
        times(total.at[:SIDE], weight, right)
        for i in range(2):
            at = 2 * i * WIDTH
            block = jnp.where(
                even, total[at : at + PADDED], total[at + WIDTH : at + WIDTH + PADDED]
            )
            if own:
                block = block + rest[9][row, i].astype(jnp.float32)
            out[row, i] = block.astype(out.dtype)


def weight_kernel(rows_first, here, slabs, hidden, out):
    right = hidden[...]
    for step in range(ROWS):
        slab = slabs[lax.rem(here[0] + step, ROWS)]
        left, other = (slab, right) if rows_first else (right, slab)
        out[step, :SIDE] = dot(left, other[:MAIN], 1, 1).astype(out.dtype)
        rest = dot(other[MAIN:], left, 1, 1).astype(out.dtype)
        out[step, SIDE : SIDE + REST] = rest[:, :MAIN]
        out[step, SIDE + REST :] = jnp.zeros((REST, MAIN), out.dtype)
        out[step, SIDE + REST :, :REST] = rest[:, MAIN:]


def call(kernel, out_shape, scratch, here, *operands):
    return pl.pallas_call(
        kernel,
        out_shape=jax.ShapeDtypeStruct(out_shape, jnp.bfloat16),
        in_specs=[pl.BlockSpec(memory_space=pltpu.SMEM)]
        + [pl.BlockSpec(memory_space=pltpu.VMEM)] * len(operands),
        out_specs=pl.BlockSpec(memory_space=pltpu.VMEM),
        scratch_shapes=[pltpu.VMEM(shape, jnp.float32) for shape in scratch],
        compiler_params=pltpu.CompilerParams(vmem_limit_bytes=40 * 2**20),
        cost_estimate=pl.CostEstimate(
            flops=2 * 4096 * SIDE * SIDE, bytes_accessed=8 * 2**20, transcendentals=0
        ),
    )(here, *operands)


def per_device(tokens, pre_act, out_grad, up_weight, down_weight):
    row, core = lax.axis_index("row"), lax.axis_index("col") % 2
    here = jnp.stack([row, core]).astype(jnp.int32)

    def to_plane(block):
        block = jnp.pad(block.T, ((0, PADDED - WIDTH), (0, 0)))
        return to_chips(jnp.broadcast_to(block[None], (CHIPS,) + block.shape))

    def all_widths(own):
        other = swap_cores(own)
        return call(order_kernel, (ROWS, SIDE, BLOCK), [(SIDE, BLOCK)], here, own, other)

    down_pieces = gather_ring(pack(down_weight))
    up_pieces = gather_ring(pack(up_weight))

    grad_own = to_plane(out_grad)
    grad_own = after(grad_own, *down_pieces[:4])
    grad_full = all_widths(grad_own)
    tok_own = to_plane(after(tokens, grad_own))
    tok_own = after(tok_own, *down_pieces)
    tok_full = all_widths(tok_own)

    act, slope = gelu_parts(pre_act.T.astype(jnp.float32))
    parts = (ROWS, PACKED, MAIN)
    down_parts = call(
        functools.partial(weight_kernel, False), parts, [], here, grad_full, act.astype(jnp.bfloat16)
    )
    pre_grad = call(
        hidden_kernel, (SIDE, BLOCK), [(SIDE, BLOCK)], here, grad_full, slope, *down_pieces
    )
    up_parts = call(functools.partial(weight_kernel, True), parts, [], here, tok_full, pre_grad)
    down_grad = sum_ring(down_parts)
    up_grad = sum_ring(up_parts)

    shape, scratch = (ROWS, 2, PADDED, BLOCK), [(SIDE + 16, BLOCK)]
    kernel = functools.partial(input_kernel, False)
    sent = swap_cores(call(kernel, shape, scratch, here, pre_grad, *up_pieces))
    kernel = functools.partial(input_kernel, True)
    pair = call(kernel, shape, scratch, here, pre_grad, *up_pieces, sent)
    moved = to_chips(pair.reshape(CHIPS, PADDED, BLOCK))
    tokens_grad = jnp.sum(moved.astype(jnp.float32), axis=0)[:WIDTH].T.astype(jnp.bfloat16)
    return (tokens_grad, up_grad, down_grad)


def solution(mesh):
    in_specs = (P("row", "col"), P("row", "col"), P("row", "col"), P("row", "col"), P("col", "row"))
    out_specs = (P("row", "col"), P("row", "col"), P("col", "row"))
    return jax.shard_map(
        per_device, mesh=mesh, in_specs=in_specs, out_specs=out_specs, check_vma=False
    )
```

```python
import functools

import jax
import jax.numpy as jnp
from jax import lax
from jax.experimental import pallas as pl
from jax.experimental.pallas import tpu as pltpu
from jax.sharding import PartitionSpec as P

INV_ROOT_TWO = 0.7071067811865476
INV_ROOT_TAU = 0.3989422804014327

ROWS = 8
COLS = 32
CHIPS = COLS // 2
BLOCK = 512
SIDE = 400
WIDTH = 100
PADDED = 112
SHORT = 104
MAIN = 384
REST = SIDE - MAIN
PACKED = SIDE + 2 * REST
HALF = 224

SAME_CORE = [[2 * chip + core for chip in range(CHIPS)] for core in range(2)]
CORE_SWAP = [(c, c ^ 1) for c in range(COLS)]
OFFSETS = (0, -1, 1, -2, 2, -3, 3)


def gelu_parts(pre_value):
    normal_cdf = 0.5 * (1.0 + lax.erf(pre_value * INV_ROOT_TWO))
    slope = normal_cdf + pre_value * jnp.exp(-0.5 * pre_value * pre_value) * INV_ROOT_TAU
    return (pre_value * normal_cdf, slope)


def after(value, *earlier):
    return lax.optimization_barrier((value,) + earlier)[0]


def shift(block, step):
    return lax.ppermute(block, "row", [(i, (i + step) % ROWS) for i in range(ROWS)])


class GatherRing:
    def __init__(self, block):
        self.ends = (block, block)
        self.pieces = [block]

    def go(self, *earlier):
        up, down = self.ends
        if earlier:
            up, down = after(up, *earlier), after(down, *earlier)
        if len(self.pieces) < 7:
            self.ends = shift(up, 1), shift(down, -1)
        else:
            self.ends = shift(up[:HALF], 1), shift(down[HALF:], -1)
        self.pieces += self.ends


def plus(part, came):
    return (part.astype(jnp.float32) + came.astype(jnp.float32)).astype(part.dtype)


class SumRing:
    def __init__(self, parts):
        self.parts = parts
        self.ends = (parts[4, :HALF], parts[4, HALF:])
        self.step = 4

    def go(self, *earlier):
        up, down = self.ends
        if earlier:
            up, down = after(up, *earlier), after(down, *earlier)
        up, down = shift(up, 1), shift(down, -1)
        self.step -= 1
        if self.step == 0:
            self.ends = up, down
            return
        above, below = self.parts[self.step], self.parts[ROWS - self.step]
        if self.step == 3:
            up = jnp.concatenate([plus(above[:HALF], up), above[HALF:]], axis=0)
            down = jnp.concatenate([below[:HALF], plus(below[HALF:], down)], axis=0)
        else:
            up, down = plus(above, up), plus(below, down)
        self.ends = up, down

    def total(self):
        up, down = (end.astype(jnp.float32) for end in self.ends)
        total = self.parts[0].astype(jnp.float32) + up + down
        rest = jnp.concatenate([total[SIDE : SIDE + REST], total[SIDE + REST :, :REST]], axis=1)
        return jnp.concatenate([total[:SIDE], rest.T], axis=1)


def pack(block):
    rest = block[:, MAIN:].T
    corner = jnp.pad(rest[:, MAIN:], ((0, 0), (0, MAIN - REST)))
    return jnp.concatenate([block[:, :MAIN], rest[:, :MAIN], corner], axis=0)


def swap_cores(block):
    return lax.ppermute(block, "col", CORE_SWAP)


def to_chips(blocks):
    flat = blocks.reshape((-1,) + blocks.shape[2:])
    moved = lax.all_to_all(flat, "col", 0, 0, tiled=True, axis_index_groups=SAME_CORE)
    return moved.reshape(blocks.shape)


def dot(left, right, left_dim, right_dim):
    return lax.dot_general(
        left,
        right,
        (((left_dim,), (right_dim,)), ((), ())),
        preferred_element_type=jnp.float32,
    )


def each_row(here, pieces):
    for offset, piece in zip(OFFSETS, pieces):
        yield lax.rem(here[0] + (offset + ROWS), ROWS), piece[...]
    far = jnp.concatenate([pieces[7][...], pieces[8][...]], axis=0)
    yield lax.rem(here[0] + 4, ROWS), far


def times(total, weight, right):
    total[...] = dot(weight[:SIDE], right[:MAIN], 1, 0)
    add_rest(total, weight, right)


def add_rest(total, weight, right):
    total[:MAIN] += dot(weight[SIDE : SIDE + REST], right[MAIN:], 0, 0)
    corner = weight[SIDE + REST :, :128]
    total[MAIN:] += dot(corner, right[MAIN:], 0, 0)[:REST]


def order_kernel(which, here, own, other, out, tall):
    first = here[1] == 0
    lanes = slice(which * BLOCK, (which + 1) * BLOCK)
    for row in range(ROWS):
        for j in range(4):
            mine, their = own[2 * row + j // 2, :, lanes], other[2 * row + j // 2, :, lanes]
            if j % 2:
                mine, their = their, mine
            block = jnp.where(first, mine.astype(jnp.float32), their.astype(jnp.float32))
            tall[j * WIDTH : (j + 1) * WIDTH] = block[:WIDTH]
        out[row] = tall[...].astype(out.dtype)


def hidden_kernel(here, grad, slope, *rest):
    pieces, (out, total) = rest[:9], rest[9:]
    total[...] = jnp.zeros_like(total)
    for row, weight in each_row(here, pieces):
        right = grad[row]
        total[...] += dot(weight[:SIDE], right[:MAIN], 1, 0)
        add_rest(total, weight, right)
    out[...] = (total[...] * slope[...]).astype(out.dtype)


def input_kernel(own, here, pre_grad, *rest):
    pieces, (out, total) = rest[:9], rest[-2:]
    even = here[1] == (0 if own else 1)
    right = pre_grad[...]
    total[SIDE:] = jnp.zeros_like(total[SIDE:])
    for row, weight in each_row(here, pieces):
        times(total.at[:SIDE], weight, right)
        for i in range(2):
            at = 2 * i * WIDTH
            block = jnp.where(
                even, total[at : at + PADDED], total[at + WIDTH : at + WIDTH + PADDED]
            )
            if own:
                block = block + rest[9][row, i].astype(jnp.float32)
            out[row, i] = block.astype(out.dtype)


def weight_kernel(rows_first, here, slabs, hidden, out):
    right = hidden[...]
    for step in range(ROWS):
        slab = slabs[lax.rem(here[0] + step, ROWS)]
        left, other = (slab, right) if rows_first else (right, slab)
        out[step, :SIDE] = dot(left, other[:MAIN], 1, 1).astype(out.dtype)
        rest = dot(other[MAIN:], left, 1, 1).astype(out.dtype)
        out[step, SIDE : SIDE + REST] = rest[:, :MAIN]
        out[step, SIDE + REST :] = jnp.zeros((REST, MAIN), out.dtype)
        out[step, SIDE + REST :, :REST] = rest[:, MAIN:]


def call(kernel, out_shape, scratch, here, *operands):
    return pl.pallas_call(
        kernel,
        out_shape=jax.ShapeDtypeStruct(out_shape, jnp.bfloat16),
        in_specs=[pl.BlockSpec(memory_space=pltpu.SMEM)]
        + [pl.BlockSpec(memory_space=pltpu.VMEM)] * len(operands),
        out_specs=pl.BlockSpec(memory_space=pltpu.VMEM),
        scratch_shapes=[pltpu.VMEM(shape, jnp.float32) for shape in scratch],
        compiler_params=pltpu.CompilerParams(vmem_limit_bytes=40 * 2**20),
        cost_estimate=pl.CostEstimate(
            flops=0, bytes_accessed=0, transcendentals=0
        ),
    )(here, *operands)


def per_device(tokens, pre_act, out_grad, up_weight, down_weight):
    row, core = lax.axis_index("row"), lax.axis_index("col") % 2
    here = jnp.stack([row, core]).astype(jnp.int32)

    def tall(block):
        return jnp.pad(block.T, ((0, SHORT - WIDTH), (0, 0)))

    both = jnp.concatenate([tall(out_grad), tall(tokens)], axis=1)
    both_own = to_chips(jnp.broadcast_to(both[None], (CHIPS,) + both.shape))
    down_ring, up_ring = GatherRing(pack(down_weight)), GatherRing(pack(up_weight))
    for _ in range(4):
        down_ring.go()
        up_ring.go()
    both_own = after(both_own, *down_ring.pieces[:7], *up_ring.pieces[:7])
    both_other = swap_cores(both_own)

    def all_widths(which):
        kernel = functools.partial(order_kernel, which)
        return call(kernel, (ROWS, SIDE, BLOCK), [(SIDE, BLOCK)], here, both_own, both_other)

    grad_full = all_widths(0)
    act, slope = gelu_parts(pre_act.T.astype(jnp.float32))
    parts = (ROWS, PACKED, MAIN)
    kernel = functools.partial(weight_kernel, False)
    down_parts = call(kernel, parts, [], here, grad_full, act.astype(jnp.bfloat16))
    down_sum = SumRing(down_parts)
    down_sum.go()
    pre_grad = call(
        hidden_kernel, (SIDE, BLOCK), [(SIDE, BLOCK)],
        here, grad_full, after(slope, down_parts), *down_ring.pieces,
    )
    tok_full = all_widths(1)
    kernel = functools.partial(weight_kernel, True)
    up_parts = call(kernel, parts, [], here, tok_full, after(pre_grad, *down_sum.ends))
    up_sum = SumRing(up_parts)

    shape, scratch = (ROWS, 2, PADDED, BLOCK), [(SIDE + 16, BLOCK)]
    kernel = functools.partial(input_kernel, False)
    sent = call(kernel, shape, scratch, here, after(pre_grad, up_parts), *up_ring.pieces)
    sent = swap_cores(sent)
    kernel = functools.partial(input_kernel, True)
    pair = call(kernel, shape, scratch, here, pre_grad, *up_ring.pieces, sent)
    moved = to_chips(pair.reshape(CHIPS, PADDED, BLOCK))
    tokens_grad = jnp.sum(moved.astype(jnp.float32), axis=0)[:WIDTH].T.astype(jnp.bfloat16)

    down_sum.go()
    up_sum.go(*down_sum.ends)
    down_sum.go()
    up_sum.go()
    down_sum.go()
    up_sum.go(pair)
    down_grad = down_sum.total()
    up_sum.go()
    up_sum.ends = lax.optimization_barrier((*up_sum.ends, tokens_grad, down_grad))[:2]
    return (tokens_grad, up_sum.total(), down_grad)


def solution(mesh):
    in_specs = (P("row", "col"), P("row", "col"), P("row", "col"), P("row", "col"), P("col", "row"))
    out_specs = (P("row", "col"), P("row", "col"), P("col", "row"))
    return jax.shard_map(
        per_device, mesh=mesh, in_specs=in_specs, out_specs=out_specs, check_vma=False
    )
```

```python
import functools

import jax
import jax.numpy as jnp
from jax import lax
from jax.experimental import pallas as pl
from jax.experimental.pallas import tpu as pltpu
from jax.sharding import PartitionSpec as P

INV_ROOT_TWO = 0.7071067811865476
INV_ROOT_TAU = 0.3989422804014327

ROWS = 8
COLS = 32
CHIPS = COLS // 2
BLOCK = 512
SIDE = 400
WIDTH = 100
PADDED = 112
SHORT = 104
MAIN = 384
REST = SIDE - MAIN
PACKED = SIDE + 2 * REST
HALF = 224

SAME_CORE = [[2 * chip + core for chip in range(CHIPS)] for core in range(2)]
CORE_SWAP = [(c, c ^ 1) for c in range(COLS)]
OFFSETS = (0, -1, 1, -2, 2, -3, 3)


def gelu_parts(pre_value):
    normal_cdf = 0.5 * (1.0 + lax.erf(pre_value * INV_ROOT_TWO))
    slope = normal_cdf + pre_value * jnp.exp(-0.5 * pre_value * pre_value) * INV_ROOT_TAU
    return (pre_value * normal_cdf, slope)


def after(value, *earlier):
    return lax.optimization_barrier((value,) + earlier)[0]


def shift(block, step):
    return lax.ppermute(block, "row", [(i, (i + step) % ROWS) for i in range(ROWS)])


class GatherRing:
    def __init__(self, block):
        self.ends = (block, block)
        self.pieces = [block]

    def go(self, *earlier):
        up, down = self.ends
        if earlier:
            up, down = after(up, *earlier), after(down, *earlier)
        if len(self.pieces) < 7:
            self.ends = shift(up, 1), shift(down, -1)
        else:
            self.ends = shift(up[:HALF], 1), shift(down[HALF:], -1)
        self.pieces += self.ends


def plus(part, came):
    return (part.astype(jnp.float32) + came.astype(jnp.float32)).astype(part.dtype)


class SumRing:
    def __init__(self, parts):
        self.parts = parts
        self.ends = (parts[4, :HALF], parts[4, HALF:])
        self.step = 4

    def go(self, *earlier):
        up, down = self.ends
        if earlier:
            up, down = after(up, *earlier), after(down, *earlier)
        up, down = shift(up, 1), shift(down, -1)
        self.step -= 1
        if self.step == 0:
            self.ends = up, down
            return
        above, below = self.parts[self.step], self.parts[ROWS - self.step]
        if self.step == 3:
            up = jnp.concatenate([plus(above[:HALF], up), above[HALF:]], axis=0)
            down = jnp.concatenate([below[:HALF], plus(below[HALF:], down)], axis=0)
        else:
            up, down = plus(above, up), plus(below, down)
        self.ends = up, down

    def total(self):
        up, down = (end.astype(jnp.float32) for end in self.ends)
        total = self.parts[0].astype(jnp.float32) + up + down
        rest = jnp.concatenate([total[SIDE : SIDE + REST], total[SIDE + REST :, :REST]], axis=1)
        return jnp.concatenate([total[:SIDE], rest.T], axis=1)


def pack(block):
    rest = block[:, MAIN:].T
    corner = jnp.pad(rest[:, MAIN:], ((0, 0), (0, MAIN - REST)))
    return jnp.concatenate([block[:, :MAIN], rest[:, :MAIN], corner], axis=0)


def swap_cores(block):
    return lax.ppermute(block, "col", CORE_SWAP)


def to_chips(blocks):
    flat = blocks.reshape((-1,) + blocks.shape[2:])
    moved = lax.all_to_all(flat, "col", 0, 0, tiled=True, axis_index_groups=SAME_CORE)
    return moved.reshape(blocks.shape)


def dot(left, right, left_dim, right_dim):
    return lax.dot_general(
        left,
        right,
        (((left_dim,), (right_dim,)), ((), ())),
        preferred_element_type=jnp.float32,
    )


def each_row(here, pieces):
    for offset, piece in zip(OFFSETS, pieces):
        yield lax.rem(here[0] + (offset + ROWS), ROWS), piece[...]
    far = jnp.concatenate([pieces[7][...], pieces[8][...]], axis=0)
    yield lax.rem(here[0] + 4, ROWS), far


def times(total, weight, right):
    total[...] = dot(weight[:SIDE], right[:MAIN], 1, 0)
    add_rest(total, weight, right)


def add_rest(total, weight, right):
    total[:MAIN] += dot(weight[SIDE : SIDE + REST], right[MAIN:], 0, 0)
    corner = weight[SIDE + REST :, :128]
    total[MAIN:] += dot(corner, right[MAIN:], 0, 0)[:REST]


def order_kernel(which, here, own, other, out, tall):
    first = here[1] == 0
    lanes = slice(which * BLOCK, (which + 1) * BLOCK)
    for row in range(ROWS):
        for j in range(4):
            mine, their = own[2 * row + j // 2, :, lanes], other[2 * row + j // 2, :, lanes]
            if j % 2:
                mine, their = their, mine
            block = jnp.where(first, mine.astype(jnp.float32), their.astype(jnp.float32))
            tall[j * WIDTH : (j + 1) * WIDTH] = block[:WIDTH]
        out[row] = tall[...].astype(out.dtype)


def hidden_kernel(here, grad, slope, *rest):
    pieces, (out, total) = rest[:9], rest[9:]
    total[...] = jnp.zeros_like(total)
    for row, weight in each_row(here, pieces):
        right = grad[row]
        total[...] += dot(weight[:SIDE], right[:MAIN], 1, 0)
        add_rest(total, weight, right)
    out[...] = (total[...] * slope[...]).astype(out.dtype)


def input_kernel(own, here, pre_grad, *rest):
    pieces, (out, total) = rest[:9], rest[-2:]
    even = here[1] == (0 if own else 1)
    right = pre_grad[...]
    total[SIDE:] = jnp.zeros_like(total[SIDE:])
    for row, weight in each_row(here, pieces):
        times(total.at[:SIDE], weight, right)
        for i in range(2):
            at = 2 * i * WIDTH
            block = jnp.where(
                even, total[at : at + PADDED], total[at + WIDTH : at + WIDTH + PADDED]
            )
            if own:
                block = block + rest[9][row, i].astype(jnp.float32)
            out[row, i] = block.astype(out.dtype)


def weight_kernel(rows_first, here, slabs, hidden, out):
    right = hidden[...]
    for step in range(ROWS):
        slab = slabs[lax.rem(here[0] + step, ROWS)]
        left, other = (slab, right) if rows_first else (right, slab)
        out[step, :SIDE] = dot(left, other[:MAIN], 1, 1).astype(out.dtype)
        rest = dot(other[MAIN:], left, 1, 1).astype(out.dtype)
        out[step, SIDE : SIDE + REST] = rest[:, :MAIN]
        out[step, SIDE + REST :] = jnp.zeros((REST, MAIN), out.dtype)
        out[step, SIDE + REST :, :REST] = rest[:, MAIN:]


def call(kernel, out_shape, scratch, here, *operands):
    return pl.pallas_call(
        kernel,
        out_shape=jax.ShapeDtypeStruct(out_shape, jnp.bfloat16),
        in_specs=[pl.BlockSpec(memory_space=pltpu.SMEM)]
        + [pl.BlockSpec(memory_space=pltpu.VMEM)] * len(operands),
        out_specs=pl.BlockSpec(memory_space=pltpu.VMEM),
        scratch_shapes=[pltpu.VMEM(shape, jnp.float32) for shape in scratch],
        compiler_params=pltpu.CompilerParams(vmem_limit_bytes=40 * 2**20),
        cost_estimate=pl.CostEstimate(
            flops=0, bytes_accessed=0, transcendentals=0
        ),
    )(here, *operands)


def per_device(tokens, pre_act, out_grad, up_weight, down_weight):
    row, core = lax.axis_index("row"), lax.axis_index("col") % 2
    here = jnp.stack([row, core]).astype(jnp.int32)

    def tall(block):
        return jnp.pad(block.T, ((0, SHORT - WIDTH), (0, 0)))

    both = jnp.concatenate([tall(out_grad), tall(tokens)], axis=1)
    both_own = to_chips(jnp.broadcast_to(both[None], (CHIPS,) + both.shape))
    down_ring, up_ring = GatherRing(pack(down_weight)), GatherRing(pack(up_weight))
    for _ in range(4):
        down_ring.go()
        up_ring.go()
    both_own = after(both_own, *down_ring.pieces[:7], *up_ring.pieces[:7])
    both_other = swap_cores(both_own)

    def all_widths(which):
        kernel = functools.partial(order_kernel, which)
        return call(kernel, (ROWS, SIDE, BLOCK), [(SIDE, BLOCK)], here, both_own, both_other)

    grad_full = all_widths(0)
    act, slope = gelu_parts(pre_act.T.astype(jnp.float32))
    parts = (ROWS, PACKED, MAIN)
    kernel = functools.partial(weight_kernel, False)
    down_parts = call(kernel, parts, [], here, grad_full, act.astype(jnp.bfloat16))
    down_sum = SumRing(down_parts)
    down_sum.go()
    pre_grad = call(
        hidden_kernel, (SIDE, BLOCK), [(SIDE, BLOCK)],
        here, grad_full, after(slope, down_parts), *down_ring.pieces,
    )
    tok_full = all_widths(1)
    kernel = functools.partial(weight_kernel, True)
    up_parts = call(kernel, parts, [], here, tok_full, after(pre_grad, *down_sum.ends))
    up_sum = SumRing(up_parts)

    shape, scratch = (ROWS, 2, PADDED, BLOCK), [(SIDE + 16, BLOCK)]
    kernel = functools.partial(input_kernel, False)
    sent = call(kernel, shape, scratch, here, pre_grad, *up_ring.pieces)
    sent = swap_cores(sent)
    kernel = functools.partial(input_kernel, True)
    pair = call(kernel, shape, scratch, here, pre_grad, *up_ring.pieces, sent)
    moved = to_chips(pair.reshape(CHIPS, PADDED, BLOCK))
    tokens_grad = jnp.sum(moved.astype(jnp.float32), axis=0)[:WIDTH].T.astype(jnp.bfloat16)

    for _ in range(3):
        down_sum.go()
        up_sum.go()
    down_grad = down_sum.total()
    up_sum.go()
    up_sum.ends = lax.optimization_barrier((*up_sum.ends, tokens_grad, down_grad))[:2]
    return (tokens_grad, up_sum.total(), down_grad)


def solution(mesh):
    in_specs = (P("row", "col"), P("row", "col"), P("row", "col"), P("row", "col"), P("col", "row"))
    out_specs = (P("row", "col"), P("row", "col"), P("col", "row"))
    return jax.shard_map(
        per_device, mesh=mesh, in_specs=in_specs, out_specs=out_specs, check_vma=False
    )
```

```python
import functools

import jax
import jax.numpy as jnp
from jax import lax
from jax.experimental import pallas as pl
from jax.experimental.pallas import tpu as pltpu
from jax.sharding import PartitionSpec as P

INV_ROOT_TWO = 0.7071067811865476
INV_ROOT_TAU = 0.3989422804014327

ROWS = 8
COLS = 32
CHIPS = COLS // 2
BLOCK = 512
SIDE = 400
WIDTH = 100
PADDED = 104
SHORT = 104
MAIN = 384
REST = SIDE - MAIN
PACKED = SIDE + 2 * REST
HALF = 224

SAME_CORE = [[2 * chip + core for chip in range(CHIPS)] for core in range(2)]
CORE_SWAP = [(c, c ^ 1) for c in range(COLS)]
OFFSETS = (0, -1, 1, -2, 2, -3, 3)


def gelu_parts(pre_value):
    normal_cdf = 0.5 * (1.0 + lax.erf(pre_value * INV_ROOT_TWO))
    slope = normal_cdf + pre_value * jnp.exp(-0.5 * pre_value * pre_value) * INV_ROOT_TAU
    return (pre_value * normal_cdf, slope)


def after(value, *earlier):
    return lax.optimization_barrier((value,) + earlier)[0]


def shift(block, step):
    return lax.ppermute(block, "row", [(i, (i + step) % ROWS) for i in range(ROWS)])


class GatherRing:
    def __init__(self, block):
        self.ends = (block, block)
        self.pieces = [block]

    def go(self, *earlier):
        up, down = self.ends
        if earlier:
            up, down = after(up, *earlier), after(down, *earlier)
        if len(self.pieces) < 7:
            self.ends = shift(up, 1), shift(down, -1)
        else:
            self.ends = shift(up[:HALF], 1), shift(down[HALF:], -1)
        self.pieces += self.ends


def plus(part, came):
    return (part.astype(jnp.float32) + came.astype(jnp.float32)).astype(part.dtype)


class SumRing:
    def __init__(self, parts):
        self.parts = parts
        self.ends = (parts[4, :HALF], parts[4, HALF:])
        self.step = 4

    def go(self, *earlier):
        up, down = self.ends
        if earlier:
            up, down = after(up, *earlier), after(down, *earlier)
        up, down = shift(up, 1), shift(down, -1)
        self.step -= 1
        if self.step == 0:
            self.ends = up, down
            return
        above, below = self.parts[self.step], self.parts[ROWS - self.step]
        if self.step == 3:
            up = jnp.concatenate([plus(above[:HALF], up), above[HALF:]], axis=0)
            down = jnp.concatenate([below[:HALF], plus(below[HALF:], down)], axis=0)
        else:
            up, down = plus(above, up), plus(below, down)
        self.ends = up, down

    def total(self):
        up, down = (end.astype(jnp.float32) for end in self.ends)
        total = self.parts[0].astype(jnp.float32) + up + down
        rest = jnp.concatenate([total[SIDE : SIDE + REST], total[SIDE + REST :, :REST]], axis=1)
        return jnp.concatenate([total[:SIDE], rest.T], axis=1)


def pack(block):
    rest = block[:, MAIN:].T
    corner = jnp.pad(rest[:, MAIN:], ((0, 0), (0, MAIN - REST)))
    return jnp.concatenate([block[:, :MAIN], rest[:, :MAIN], corner], axis=0)


def swap_cores(block):
    return lax.ppermute(block, "col", CORE_SWAP)


def to_chips(blocks):
    flat = blocks.reshape((-1,) + blocks.shape[2:])
    moved = lax.all_to_all(flat, "col", 0, 0, tiled=True, axis_index_groups=SAME_CORE)
    return moved.reshape(blocks.shape)


def dot(left, right, left_dim, right_dim):
    return lax.dot_general(
        left,
        right,
        (((left_dim,), (right_dim,)), ((), ())),
        preferred_element_type=jnp.float32,
    )


def each_row(here, pieces):
    for offset, piece in zip(OFFSETS, pieces):
        yield lax.rem(here[0] + (offset + ROWS), ROWS), piece[...]
    far = jnp.concatenate([pieces[7][...], pieces[8][...]], axis=0)
    yield lax.rem(here[0] + 4, ROWS), far


def times(total, weight, right):
    total[...] = dot(weight[:SIDE], right[:MAIN], 1, 0)
    add_rest(total, weight, right)


def add_rest(total, weight, right):
    total[:MAIN] += dot(weight[SIDE : SIDE + REST], right[MAIN:], 0, 0)
    corner = weight[SIDE + REST :, :128]
    total[MAIN:] += dot(corner, right[MAIN:], 0, 0)[:REST]


def order_kernel(which, here, own, other, out, tall):
    first = here[1] == 0
    lanes = slice(which * BLOCK, (which + 1) * BLOCK)
    for row in range(ROWS):
        for j in range(4):
            mine, their = own[2 * row + j // 2, :, lanes], other[2 * row + j // 2, :, lanes]
            if j % 2:
                mine, their = their, mine
            block = jnp.where(first, mine.astype(jnp.float32), their.astype(jnp.float32))
            tall[j * WIDTH : (j + 1) * WIDTH] = block[:WIDTH]
        out[row] = tall[...].astype(out.dtype)


def hidden_kernel(here, grad, slope, *rest):
    pieces, (out, total) = rest[:9], rest[9:]
    total[...] = jnp.zeros_like(total)
    for row, weight in each_row(here, pieces):
        right = grad[row]
        total[...] += dot(weight[:SIDE], right[:MAIN], 1, 0)
        add_rest(total, weight, right)
    out[...] = (total[...] * slope[...]).astype(out.dtype)


def input_kernel(own, here, pre_grad, *rest):
    pieces, (out, total) = rest[:9], rest[-2:]
    even = here[1] == (0 if own else 1)
    right = pre_grad[...]
    total[SIDE:] = jnp.zeros_like(total[SIDE:])
    for row, weight in each_row(here, pieces):
        times(total.at[:SIDE], weight, right)
        for i in range(2):
            at = 2 * i * WIDTH
            block = jnp.where(
                even, total[at : at + PADDED], total[at + WIDTH : at + WIDTH + PADDED]
            )
            if own:
                block = block + rest[9][row, i].astype(jnp.float32)
            out[row, i] = block.astype(out.dtype)


def weight_kernel(rows_first, here, slabs, hidden, out):
    right = hidden[...]
    for step in range(ROWS):
        slab = slabs[lax.rem(here[0] + step, ROWS)]
        left, other = (slab, right) if rows_first else (right, slab)
        out[step, :SIDE] = dot(left, other[:MAIN], 1, 1).astype(out.dtype)
        rest = dot(other[MAIN:], left, 1, 1).astype(out.dtype)
        out[step, SIDE : SIDE + REST] = rest[:, :MAIN]
        out[step, SIDE + REST :] = jnp.zeros((REST, MAIN), out.dtype)
        out[step, SIDE + REST :, :REST] = rest[:, MAIN:]


def call(kernel, out_shape, scratch, here, *operands):
    return pl.pallas_call(
        kernel,
        out_shape=jax.ShapeDtypeStruct(out_shape, jnp.bfloat16),
        in_specs=[pl.BlockSpec(memory_space=pltpu.SMEM)]
        + [pl.BlockSpec(memory_space=pltpu.VMEM)] * len(operands),
        out_specs=pl.BlockSpec(memory_space=pltpu.VMEM),
        scratch_shapes=[pltpu.VMEM(shape, jnp.float32) for shape in scratch],
        compiler_params=pltpu.CompilerParams(vmem_limit_bytes=40 * 2**20),
        cost_estimate=pl.CostEstimate(
            flops=0, bytes_accessed=0, transcendentals=0
        ),
    )(here, *operands)


def per_device(tokens, pre_act, out_grad, up_weight, down_weight):
    row, core = lax.axis_index("row"), lax.axis_index("col") % 2
    here = jnp.stack([row, core]).astype(jnp.int32)

    def tall(block):
        return jnp.pad(block.T, ((0, SHORT - WIDTH), (0, 0)))

    both = jnp.concatenate([tall(out_grad), tall(tokens)], axis=1)
    both_own = to_chips(jnp.broadcast_to(both[None], (CHIPS,) + both.shape))
    down_ring, up_ring = GatherRing(pack(down_weight)), GatherRing(pack(up_weight))
    for _ in range(4):
        down_ring.go()
        up_ring.go()
    both_own = after(both_own, *down_ring.pieces[:7], *up_ring.pieces[:7])
    both_other = swap_cores(both_own)

    def all_widths(which):
        kernel = functools.partial(order_kernel, which)
        return call(kernel, (ROWS, SIDE, BLOCK), [(SIDE, BLOCK)], here, both_own, both_other)

    grad_full = all_widths(0)
    act, slope = gelu_parts(pre_act.T.astype(jnp.float32))
    parts = (ROWS, PACKED, MAIN)
    kernel = functools.partial(weight_kernel, False)
    down_parts = call(kernel, parts, [], here, grad_full, act.astype(jnp.bfloat16))
    down_sum = SumRing(down_parts)
    down_sum.go()
    pre_grad = call(
        hidden_kernel, (SIDE, BLOCK), [(SIDE, BLOCK)],
        here, grad_full, after(slope, down_parts), *down_ring.pieces,
    )
    tok_full = all_widths(1)
    kernel = functools.partial(weight_kernel, True)
    up_parts = call(kernel, parts, [], here, tok_full, after(pre_grad, *down_sum.ends))
    up_sum = SumRing(up_parts)

    shape, scratch = (ROWS, 2, PADDED, BLOCK), [(SIDE + 16, BLOCK)]
    kernel = functools.partial(input_kernel, False)
    sent = call(kernel, shape, scratch, here, pre_grad, *up_ring.pieces)
    sent = swap_cores(sent)
    kernel = functools.partial(input_kernel, True)
    pair = call(kernel, shape, scratch, here, pre_grad, *up_ring.pieces, sent)
    moved = to_chips(pair.reshape(CHIPS, PADDED, BLOCK))
    tokens_grad = jnp.sum(moved.astype(jnp.float32), axis=0)[:WIDTH].T.astype(jnp.bfloat16)

    for _ in range(3):
        down_sum.go()
        up_sum.go()
    down_grad = down_sum.total()
    up_sum.go()
    up_sum.ends = lax.optimization_barrier((*up_sum.ends, tokens_grad, down_grad))[:2]
    return (tokens_grad, up_sum.total(), down_grad)


def solution(mesh):
    in_specs = (P("row", "col"), P("row", "col"), P("row", "col"), P("row", "col"), P("col", "row"))
    out_specs = (P("row", "col"), P("row", "col"), P("col", "row"))
    return jax.shard_map(
        per_device, mesh=mesh, in_specs=in_specs, out_specs=out_specs, check_vma=False
    )
```
